256 devices in a mesh: rows: 128 (over y_lo, z, x, core), sub: 2 (over y_hi).
Axes of the slice: x: 4, y: 4 (y_hi: 2, y_lo: 2; y = y_hi * 2 + y_lo), z: 8, core: 2. Of those that a mesh axis runs over, the one named last changes fastest.
Arguments:
- features: bfloat16 [440, 1048576], P(None, ('rows', 'sub')), may hold values from -6 to 6
- residual: float32 [147, 1048576], P(None, ('rows', 'sub')), may hold values from -6 to 6
- coeffs: float32 [147, 1048576], P(None, ('rows', 'sub')), may hold values from -6 to 6
- inverse: float32 [2, 512, 512], replicated, may hold values from -0.25 to 0.25
- owner: int32 [2], replicated, may hold values from 0 to 255
- offsets: int32 [2, 512], replicated, may hold values from 0 to 4095, as said below
Outputs:
- new_residual: float32 [147, 1048576], P(None, ('rows', 'sub'))
- new_coeffs: float32 [147, 1048576], P(None, ('rows', 'sub'))
The draws below stay inside these ranges and needn't reach their ends.
Inputs may be any that keep to these rules, and one draw needn't show every extreme that they name: Within one step the 512 offsets are distinct; each step holds both 0 and 4095.
All inputs are finite; a program needn't handle non-finite values.
Results may differ from the reference program's by a relative error of at most 0.0038.
Values may be sent and summed in bfloat16 or wider, within the bound.
No kernel may reach another device: no remote copies, remote signals or barrier semaphores. Data moves between devices by JAX's collectives and lax.ppermute only.
A program may use at most 128 MiB of HBM per device.

```python
import jax
import jax.numpy as jnp
from jax import lax

F = 440
C = 147
B = 512
STEPS = 2
R_DEV = 4096
N = 1048576


def one_step(key):
    first_key, second_key = jax.random.split(key)
    inner = 1 + jax.random.permutation(first_key, R_DEV - 2)[:B - 2]
    values = jnp.concatenate([jnp.array([0, R_DEV - 1], dtype=jnp.int32), inner.astype(jnp.int32)])
    order = jax.random.permutation(second_key, B)
    return jnp.take(values, order)


def draw_offsets(key, part):
    key = jax.random.fold_in(key, 7)
    keys = jax.random.split(key, STEPS)
    return jax.vmap(one_step)(keys).astype(jnp.int32)


def level_of(rng, dims, cuts, low, top_value):
    def one(position, blocks):
        steps = jax.random.uniform(jax.random.fold_in(jax.random.fold_in(rng, 6), position), (blocks,), jnp.float32, low / len(cuts), top_value / len(cuts))
        return jnp.repeat(jnp.exp(steps), dims[position] // blocks).reshape((-1,) + (1,) * (len(dims) - position - 1))

    level = one(*cuts[0])
    for cut in cuts[1:]:
        level = level * one(*cut)
    return level


def bell_draw(rng, extent, scale, reach, cuts=(), kind=jnp.bfloat16):
    values = scale * jax.random.normal(rng, extent, jnp.float32)
    if cuts:
        values = values * level_of(rng, extent, cuts, -0.22, 0.18)
    return jnp.clip(values, -reach, reach).astype(kind)


def setup_inputs(seed: int = 0) -> dict:
    key_of = jax.random.split(jax.random.key(seed), 7)
    return {
        "features": bell_draw(key_of[0], (F, N), 1.0, 6.0, ((1, 256),)),
        "residual": bell_draw(key_of[1], (C, N), 1.0, 6.0, ((1, 256),), jnp.float32),
        "coeffs": bell_draw(key_of[2], (C, N), 1.0, 6.0, ((1, 256),), jnp.float32),
        "inverse": bell_draw(key_of[3], (STEPS, B, B), B ** -0.5, 0.25, (), jnp.float32),
        "owner": jax.random.randint(key_of[4], (STEPS,), 0, R_DEV // R_DEV * N // R_DEV).astype(jnp.int32),
        "offsets": draw_offsets(jax.random.fold_in(key_of[6], 71), 0),
    }


def kernel_rows(rows_feat, block):
    dots = jnp.dot(rows_feat.T, block, preferred_element_type=jnp.float32)
    rows_sq = jnp.sum(rows_feat.astype(jnp.float32) ** 2, axis=0)
    block_sq = jnp.sum(block.astype(jnp.float32) ** 2, axis=0)
    dist = rows_sq[:, None] + block_sq[None, :] - 2.0 * dots
    return jnp.exp(-2.0 * dist / rows_feat.shape[0]).astype(jnp.bfloat16)


def reference(features, residual, coeffs, inverse, owner, offsets):
    shards = N // R_DEV
    for step in range(STEPS):
        cols = (owner[step] * R_DEV + offsets[step]).astype(jnp.int32)
        block = jnp.take(features, cols, axis=1)
        delta = jnp.dot(jnp.take(residual, cols, axis=1), inverse[step], precision=lax.Precision.HIGHEST).astype(jnp.bfloat16)

        def shard_update(index):
            start = (index * R_DEV).astype(jnp.int32)
            piece = lax.dynamic_slice_in_dim(features, start, R_DEV, 1)
            kernel = kernel_rows(piece, block)
            return lax.dot_general(delta, kernel, (((1,), (1,)), ((), ())), preferred_element_type=jnp.float32)

        updates = lax.map(shard_update, jnp.arange(shards, dtype=jnp.int32))
        updates = jnp.transpose(updates, (1, 0, 2)).reshape(C, N)
        residual = residual - updates
        residual = residual.at[:, cols].add(-0.5 * delta.astype(jnp.float32))
        coeffs = coeffs.at[:, cols].add(delta.astype(jnp.float32))
    return residual, coeffs
```

```python
import math

import jax
import jax.numpy as jnp
from jax import lax
from jax.experimental import pallas as pl
from jax.experimental.pallas import tpu as pltpu
from jax.sharding import Mesh, PartitionSpec as P

STEPS = 2
F, C, B, R = 440, 147, 512, 4096
FP, CP = 448, 160
ROWS = 768
HALF = 256
GROUPS = 32
PIECE = 48
KT = 512
TILE = 512
AXES = ("yl", "zh", "zl", "x", "c", "yh")
SPREAD = ("yl", "zl", "x", "yh")
BF, F32 = jnp.bfloat16, jnp.float32
HIGH = lax.Precision.HIGHEST


def split(value, terms):
    parts = []
    for _ in range(terms):
        part = value.astype(BF)
        parts.append(part)
        value = value - part.astype(F32)
    return parts


def dot(a, b):
    return jnp.dot(a, b, preferred_element_type=F32)


def pick_kernel(info, feat, res, inv, offs, own, sib, left, acc, msg):
    tile = pl.program_id(0)
    last = pl.num_programs(0) - 1
    for step in range(STEPS):

        @pl.when(info[step] == 1)
        def _():
            left[:F, :] = feat[...]
            for i, part in enumerate(split(res[...], 3)):
                left[FP + i * CP : FP + i * CP + C, :] = part
            row = lax.broadcasted_iota(jnp.int32, (KT, B), 0) + tile * KT
            hot = jnp.where(row == offs[step : step + 1, :], 1.0, 0.0).astype(BF)
            found = dot(left[...], hot)

            @pl.when(tile == 0)
            def _():
                acc[step] = found

            @pl.when(tile > 0)
            def _():
                acc[step] += found

        @pl.when((info[step] == 1) & (tile == last))
        def _():
            msg[:FP, :] = acc[step, :FP, :].astype(BF)
            cols = acc[step, FP : FP + C, :] + (
                acc[step, FP + CP : FP + CP + C, :] + acc[step, FP + 2 * CP : FP + 2 * CP + C, :]
            )
            prod = jnp.dot(cols, inv[step], precision=HIGH, preferred_element_type=F32)
            parts = split(prod, 2)
            msg[FP : FP + C, :] = parts[0]
            if step == 1:
                msg[FP + CP : FP + CP + C, :] = parts[1]
            mine = info[2]
            for out, half in ((own, mine), (sib, 1 - mine)):
                for cb in range(2):
                    lanes = pl.ds(pl.multiple_of(half * HALF + cb * 128, 128), 128)
                    for rg in range(16):
                        out[cb * 16 + rg, PIECE * step : PIECE * (step + 1), :] = msg[
                            rg * PIECE : (rg + 1) * PIECE, lanes
                        ]


def pick(info, features, residual, inverse, offsets):
    whole = lambda *shape: pl.BlockSpec(shape, lambda i, info: (0,) * len(shape))
    piece = jax.ShapeDtypeStruct((GROUPS, 2 * PIECE, 128), BF)
    return pl.pallas_call(
        pick_kernel,
        grid_spec=pltpu.PrefetchScalarGridSpec(
            num_scalar_prefetch=1,
            grid=(R // KT,),
            in_specs=[
                pl.BlockSpec((F, KT), lambda i, info: (0, i)),
                pl.BlockSpec((C, KT), lambda i, info: (0, i)),
                whole(STEPS, B, B),
                whole(STEPS, B),
            ],
            out_specs=[whole(GROUPS, 2 * PIECE, 128)] * 2,
            scratch_shapes=[
                pltpu.VMEM((FP + 3 * CP, KT), BF),
                pltpu.VMEM((STEPS, FP + 3 * CP, B), F32),
                pltpu.VMEM((ROWS, B), BF),
            ],
        ),
        out_shape=[piece, piece],
        compiler_params=pltpu.CompilerParams(vmem_limit_bytes=48 * 1024 * 1024),
        name="pick",
    )(info, features, residual, inverse, offsets)


def update_kernel(
    info, own, sib, feat, res, coef, inv, offs, offs_col, new_res, new_coef, blk, right, blkt, delta
):
    scale = 4.0 * math.log2(math.e) / F
    mine = info[2]

    def kernel_of(lhs, rhs):
        return jnp.exp2(dot(lhs, rhs) * scale).astype(BF)

    @pl.when(pl.program_id(0) == 0)
    def _():
        for src, half in ((own, mine), (sib, 1 - mine)):
            for cb in range(2):
                lanes = pl.ds(pl.multiple_of(half * HALF + cb * 128, 128), 128)
                for rg in range(16):
                    for step in range(STEPS):
                        blk[step, rg * PIECE : (rg + 1) * PIECE, lanes] = src[
                            cb * 16 + rg, PIECE * step : PIECE * (step + 1), :
                        ]
        ones = jnp.ones((3, B), BF)
        for step in range(STEPS):
            wide = blk[step, :F, :].astype(F32)
            norm = split(-0.5 * jnp.sum(wide * wide, axis=0, keepdims=True), 3)
            zero = jnp.zeros((2, B), F32)
            tail = [part.astype(F32) for part in norm] + [jnp.ones((3, B), F32), zero]
            full = jnp.concatenate([wide] + tail, axis=0)
            blkt[step * B : (step + 1) * B, :] = full.T.astype(BF)
            if step == 1:
                tail = [jnp.ones((3, B), F32)] + [part.astype(F32) for part in norm] + [zero]
                right[:, :B] = jnp.concatenate([wide] + tail, axis=0).astype(BF)
        first = blk[0, FP : FP + C, :]
        delta[:, :B] = first
        change = dot(first, kernel_of(blkt[:B, :], right[:, :B]))
        same = (offs_col[:, 0:1] == offs[1:2, :]) & (info[3] == 1)
        change = change + dot(first, jnp.where(same, 0.5, 0.0).astype(BF))
        base = blk[1, FP : FP + C, :].astype(F32) + blk[1, FP + CP : FP + CP + C, :].astype(F32)
        after = base - jnp.dot(change, inv[1], precision=HIGH, preferred_element_type=F32)
        delta[:, B:] = after.astype(BF)

    right[:F, :] = feat[...]
    wide = feat[...].astype(F32)
    norm = split(-0.5 * jnp.sum(wide * wide, axis=0, keepdims=True), 3)
    tail = [jnp.ones((3, TILE), F32)] + [part.astype(F32) for part in norm]
    right[F:, :] = jnp.concatenate(tail + [jnp.zeros((2, TILE), F32)], axis=0).astype(BF)
    left = delta[...]
    new_res[...] = res[...] - dot(left, kernel_of(blkt[...], right[...]))
    new_coef[...] = coef[...]
    for step in range(STEPS):

        @pl.when(info[step] == 1)
        def _():
            col = lax.broadcasted_iota(jnp.int32, (B, TILE), 1) + pl.program_id(0) * TILE
            hot = jnp.where(col == offs_col[:, step : step + 1], 1.0, 0.0).astype(BF)
            placed = dot(delta[:, step * B : (step + 1) * B], hot)
            new_res[...] -= 0.5 * placed
            new_coef[...] += placed


def update(info, own, sib, features, residual, coeffs, inverse, offsets):
    whole = lambda *shape: pl.BlockSpec(shape, lambda i, info: (0,) * len(shape))
    tiles = lambda rows: pl.BlockSpec((rows, TILE), lambda i, info: (0, i))
    out = jax.ShapeDtypeStruct((C, R), F32)
    return pl.pallas_call(
        update_kernel,
        grid_spec=pltpu.PrefetchScalarGridSpec(
            num_scalar_prefetch=1,
            grid=(R // TILE,),
            in_specs=[
                whole(GROUPS, 2 * PIECE, 128),
                whole(GROUPS, 2 * PIECE, 128),
                tiles(F),
                tiles(C),
                tiles(C),
                whole(STEPS, B, B),
                whole(STEPS, B),
                whole(B, STEPS),
            ],
            out_specs=[tiles(C), tiles(C)],
            scratch_shapes=[
                pltpu.VMEM((STEPS, ROWS, B), BF),
                pltpu.VMEM((FP, TILE), BF),
                pltpu.VMEM((STEPS * B, FP), BF),
                pltpu.VMEM((C, STEPS * B), BF),
            ],
        ),
        out_shape=[out, out],
        compiler_params=pltpu.CompilerParams(vmem_limit_bytes=48 * 1024 * 1024),
        name="update",
    )(info, own, sib, features, residual, coeffs, inverse, offsets, offsets.T)


def chosen(stack, first, second):
    return jnp.concatenate(
        [
            lax.dynamic_index_in_dim(stack, first, 0, False)[:PIECE],
            lax.dynamic_index_in_dim(stack, second, 0, False)[PIECE:],
        ],
        axis=0,
    )


def exchange(piece, axes, count):
    copies = jnp.broadcast_to(piece[None], (count,) + piece.shape)
    return lax.all_to_all(copies, axes, 0, 0, tiled=True)


def shards(features, residual, coeffs, inverse, owner, offsets):
    me = lax.axis_index(AXES)
    core = lax.axis_index("c")
    same = (owner[0] == owner[1]).astype(jnp.int32)
    holds = (owner == me).astype(jnp.int32)
    info = jnp.stack([holds[0], holds[1], core, same])
    o_yh, o_c, o_x = owner % 2, owner // 2 % 2, owner // 4 % 4
    o_zl, o_zh, o_yl = owner // 16 % 2, owner // 32 % 4, owner // 128
    group = ((o_yl * 2 + o_zl) * 4 + o_x) * 2 + o_yh

    own, sib = pick(info, features, residual, inverse, offsets)
    got = lax.ppermute(sib, "c", [(0, 1), (1, 0)])
    rows = lax.broadcasted_iota(jnp.int32, own.shape, 1)
    here = jnp.where(rows < PIECE, o_c[0], o_c[1]) == core
    half = jnp.where(here, own, got)
    part = chosen(lax.all_to_all(half, SPREAD, 0, 0, tiled=True), group[0], group[1])
    part = chosen(exchange(part, "zh", 4), o_zh[0], o_zh[1])
    own = exchange(part, SPREAD, GROUPS)
    sib = lax.ppermute(own, "c", [(0, 1), (1, 0)])
    return update(info, own, sib, features, residual, coeffs, inverse, offsets)


def solution(mesh):
    fine = Mesh(mesh.devices.reshape(2, 4, 2, 4, 2, 2), AXES)
    cols = P(None, AXES)
    return jax.shard_map(
        shards,
        mesh=fine,
        in_specs=(cols, cols, cols, P(), P(), P()),
        out_specs=(cols, cols),
        check_vma=False,
    )
```

```python
import functools
import math

import jax
import jax.numpy as jnp
from jax import lax
from jax.experimental import pallas as pl
from jax.experimental.pallas import tpu as pltpu
from jax.sharding import Mesh, PartitionSpec as P

STEPS = 2
F, C, B, R = 440, 147, 512, 4096
FP, CP = 448, 160
ROWS = 768
HALF = 256
GROUPS = 32
PIECE = 48
KT = 1024
TILE = 512
AXES = ("yl", "zh", "zl", "x", "c", "yh")
SPREAD = ("yl", "zl", "x", "yh")
BF, F32 = jnp.bfloat16, jnp.float32
HIGH = lax.Precision.HIGHEST


def split(value, terms):
    parts = []
    for _ in range(terms):
        part = value.astype(BF)
        parts.append(part)
        value = value - part.astype(F32)
    return parts


def dot(a, b):
    return jnp.dot(a, b, preferred_element_type=F32)


def norm_rows(wide, first):
    terms = split(-0.5 * jnp.sum(wide * wide, axis=0, keepdims=True), 3)
    norms = [part.astype(F32) for part in terms]
    ones = [jnp.ones((3, wide.shape[1]), F32)]
    rest = [jnp.zeros((2, wide.shape[1]), F32)]
    return jnp.concatenate((norms + ones if first else ones + norms) + rest, axis=0).astype(BF)


def whole_vmem():
    return pl.BlockSpec(memory_space=pltpu.VMEM)


def in_hbm():
    return pl.BlockSpec(memory_space=pltpu.HBM)


def stay(*arrays):
    return [pltpu.with_memory_space_constraint(a, pltpu.HBM) for a in arrays]


def in_smem():
    return pl.BlockSpec(memory_space=pltpu.SMEM)


def parts_of(owner):
    group = ((owner // 128 * 2 + owner // 16 % 2) * 4 + owner // 4 % 4) * 2 + owner % 2
    return group, owner // 32 % 4, owner // 2 % 2


def pick_kernel(owner, feat, res, inv, offs, own, sib, ffeat, fres, finv, foffs, left, acc, msg, sems):
    me = lax.axis_index(AXES)
    core = lax.axis_index("c")
    chunks = R // KT

    for step in range(STEPS):

        @pl.when(owner[step] == me)
        def _():
            copies = []
            first = pltpu.make_async_copy(offs, foffs, sems.at[2 * chunks])
            last = pltpu.make_async_copy(inv.at[step], finv, sems.at[2 * chunks + 1])
            first.start()
            for i in range(chunks):
                cols = pl.ds(i * KT, KT)
                one = pltpu.make_async_copy(feat.at[:, cols], ffeat.at[:, cols], sems.at[2 * i])
                two = pltpu.make_async_copy(res.at[:, cols], fres.at[:, cols], sems.at[2 * i + 1])
                one.start()
                two.start()
                copies.append((one, two))
            last.start()
            first.wait()
            for i in range(chunks):
                for copy in copies[i]:
                    copy.wait()
                cols = pl.ds(i * KT, KT)
                left[:F, :] = ffeat[:, cols]
                for k, part in enumerate(split(fres[:, cols], 3)):
                    left[FP + k * CP : FP + k * CP + C, :] = part
                row = lax.broadcasted_iota(jnp.int32, (KT, B), 0) + i * KT
                hot = jnp.where(row == foffs[step : step + 1, :], 1.0, 0.0).astype(BF)
                found = dot(left[...], hot)
                if i == 0:
                    acc[...] = found
                else:
                    acc[...] += found
            wide = acc[:F, :]
            msg[:F, :] = wide.astype(BF)
            msg[F:FP, :] = norm_rows(wide, True)
            cols = acc[FP : FP + C, :] + (
                acc[FP + CP : FP + CP + C, :] + acc[FP + 2 * CP : FP + 2 * CP + C, :]
            )
            last.wait()
            prod = jnp.dot(cols, finv[...], precision=HIGH, preferred_element_type=F32)
            parts = split(prod, 2)
            msg[FP : FP + C, :] = parts[0]
            if step == 1:
                msg[FP + CP : FP + CP + C, :] = parts[1]
            for out, half in ((own, core), (sib, 1 - core)):
                for cb in range(2):
                    lanes = pl.ds(pl.multiple_of(half * HALF + cb * 128, 128), 128)
                    for rg in range(16):
                        out[cb * 16 + rg, PIECE * step : PIECE * (step + 1), :] = msg[
                            rg * PIECE : (rg + 1) * PIECE, lanes
                        ]


def pick(owner, features, residual, inverse, offsets):
    piece = jax.ShapeDtypeStruct((GROUPS, 2 * PIECE, 128), BF)
    return pl.pallas_call(
        pick_kernel,
        in_specs=[in_smem()] + [in_hbm()] * 4,
        out_specs=[whole_vmem()] * 2,
        scratch_shapes=[
            pltpu.VMEM((F, R), BF),
            pltpu.VMEM((C, R), F32),
            pltpu.VMEM((B, B), F32),
            pltpu.VMEM((STEPS, B), jnp.int32),
            pltpu.VMEM((FP + 3 * CP, KT), BF),
            pltpu.VMEM((FP + 3 * CP, B), F32),
            pltpu.VMEM((ROWS, B), BF),
            pltpu.SemaphoreType.DMA((2 * (R // KT) + 2,)),
        ],
        out_shape=[piece, piece],
        compiler_params=pltpu.CompilerParams(vmem_limit_bytes=20 * 1024 * 1024),
        name="pick",
    )(owner, *stay(features, residual, inverse, offsets))


def half_kernel(owner, own, got, out):
    core = lax.axis_index("c")
    for step in range(STEPS):
        rows = slice(PIECE * step, PIECE * (step + 1))
        here = owner[step] // 2 % 2 == core

        @pl.when(here)
        def _():
            out[:, rows, :] = own[:, rows, :]

        @pl.when(jnp.logical_not(here))
        def _():
            out[:, rows, :] = got[:, rows, :]


def choose_kernel(which, owner, stack, out):
    for step in range(STEPS):
        rows = slice(PIECE * step, PIECE * (step + 1))
        piece = stack[parts_of(owner[step])[which], rows, :]
        for i in range(out.shape[0]):
            out[i, rows, :] = piece


def small(kernel, count, owner, *arrays):
    return pl.pallas_call(
        kernel,
        in_specs=[in_smem()] + [whole_vmem()] * len(arrays),
        out_specs=whole_vmem(),
        out_shape=jax.ShapeDtypeStruct((count, 2 * PIECE, 128), BF),
        compiler_params=pltpu.CompilerParams(vmem_limit_bytes=4 * 1024 * 1024),
        name="choose",
    )(owner, *arrays)


def update_kernel(
    owner, own, sib, feat, res, coef, inv, offs, offs_col, new_res, new_coef,
    vfeat, vres, vcoef, vinv, voffs, vcol, blk, blkt, right, delta, sems, out_sems,
):
    scale = 4.0 * math.log2(math.e) / F
    me = lax.axis_index(AXES)
    mine = lax.axis_index("c")
    tiles = R // TILE
    holds = [owner[step] == me for step in range(STEPS)]

    def cols(i):
        return pl.ds(pl.multiple_of(i * TILE, TILE), TILE)

    def load_feat(i):
        return pltpu.make_async_copy(feat.at[:, cols(i)], vfeat.at[:, cols(i)], sems.at[i])

    def load_res(i):
        return pltpu.make_async_copy(res.at[:, cols(i)], vres.at[:, cols(i)], sems.at[tiles + i])

    def store_res(i):
        return pltpu.make_async_copy(vres.at[:, cols(i)], new_res.at[:, cols(i)], out_sems.at[i])

    def store_coef(i):
        return pltpu.make_async_copy(vcoef.at[:, cols(i)], new_coef.at[:, cols(i)], out_sems.at[tiles + i])

    load_inv = pltpu.make_async_copy(inv.at[1], vinv, sems.at[2 * tiles])
    load_offs = pltpu.make_async_copy(offs, voffs, sems.at[2 * tiles + 1])
    load_col = pltpu.make_async_copy(offs_col, vcol, sems.at[2 * tiles + 2])
    load_coef = pltpu.make_async_copy(coef, vcoef, sems.at[2 * tiles + 3])
    load_inv.start()
    for i in range(tiles):
        load_feat(i).start()
        load_res(i).start()

    load_coef.start()
    load_offs.start()
    load_col.start()

    def kernel_of(lhs, rhs):
        return jnp.exp2(dot(lhs, rhs) * scale).astype(BF)

    for src, half in ((own, mine), (sib, 1 - mine)):
        for cb in range(2):
            lanes = pl.ds(pl.multiple_of(half * HALF + cb * 128, 128), 128)
            for rg in range(16):
                for step in range(STEPS):
                    blk[step, rg * PIECE : (rg + 1) * PIECE, lanes] = src[
                        cb * 16 + rg, PIECE * step : PIECE * (step + 1), :
                    ]
    for step in range(STEPS):
        blkt[step * B : (step + 1) * B, :] = blk[step, :FP, :].astype(F32).T.astype(BF)
    right[:F, :B] = blk[1, :F, :]
    right[F:, :B] = norm_rows(blk[1, :F, :].astype(F32), False)
    first = blk[0, FP : FP + C, :]
    delta[:, :B] = first
    change = dot(first, kernel_of(blkt[:B, :], right[:, :B]))
    load_offs.wait()
    load_col.wait()
    same = (vcol[:, 0:1] == voffs[1:2, :]) & (owner[0] == owner[1])
    change = change + dot(first, jnp.where(same, 0.5, 0.0).astype(BF))
    base = blk[1, FP : FP + C, :].astype(F32) + blk[1, FP + CP : FP + CP + C, :].astype(F32)
    load_inv.wait()
    after = base - jnp.dot(change, vinv[...], precision=HIGH, preferred_element_type=F32)
    delta[:, B:] = after.astype(BF)

    load_coef.wait()

    def body(i, carry):
        load_feat(i).wait()
        load_res(i).wait()
        tile = vfeat[:, cols(i)]
        right[:F, :] = tile
        right[F:, :] = norm_rows(tile.astype(F32), False)
        vres[:, cols(i)] -= dot(delta[...], kernel_of(blkt[...], right[...]))

        for step in range(STEPS):

            @pl.when(holds[step])
            def _():
                col = lax.broadcasted_iota(jnp.int32, (B, TILE), 1) + i * TILE
                hot = jnp.where(col == vcol[:, step : step + 1], 1.0, 0.0).astype(BF)
                placed = dot(delta[:, step * B : (step + 1) * B], hot)
                vres[:, cols(i)] -= 0.5 * placed
                vcoef[:, cols(i)] += placed

        store_res(i).start()
        store_coef(i).start()
        return carry

    lax.fori_loop(0, tiles, body, 0)
    for i in range(tiles):
        store_res(i).wait()
        store_coef(i).wait()


def update(owner, own, sib, features, residual, coeffs, inverse, offsets):
    out = jax.ShapeDtypeStruct((C, R), F32)
    tiles = R // TILE
    return pl.pallas_call(
        update_kernel,
        in_specs=[in_smem()] + [whole_vmem()] * 2 + [in_hbm()] * 6,
        out_specs=[in_hbm()] * 2,
        scratch_shapes=[
            pltpu.VMEM((F, R), BF),
            pltpu.VMEM((C, R), F32),
            pltpu.VMEM((C, R), F32),
            pltpu.VMEM((B, B), F32),
            pltpu.VMEM((STEPS, B), jnp.int32),
            pltpu.VMEM((B, STEPS), jnp.int32),
            pltpu.VMEM((STEPS, ROWS, B), BF),
            pltpu.VMEM((STEPS * B, FP), BF),
            pltpu.VMEM((FP, TILE), BF),
            pltpu.VMEM((C, STEPS * B), BF),
            pltpu.SemaphoreType.DMA((2 * tiles + 4,)),
            pltpu.SemaphoreType.DMA((2 * tiles,)),
        ],
        out_shape=[out, out],
        compiler_params=pltpu.CompilerParams(vmem_limit_bytes=24 * 1024 * 1024),
        name="update",
    )(owner, own, sib, *stay(features, residual, coeffs, inverse, offsets, offsets.T))


def shards(features, residual, coeffs, inverse, owner, offsets):
    swap = [(0, 1), (1, 0)]
    owner = pltpu.with_memory_space_constraint(owner, pltpu.SMEM)
    own, sib = pick(owner, features, residual, inverse, offsets)
    half = small(half_kernel, GROUPS, owner, own, lax.ppermute(sib, "c", swap))
    part = lax.all_to_all(half, SPREAD, 0, 0, tiled=True)
    part = small(functools.partial(choose_kernel, 0), 4, owner, part)
    part = lax.all_to_all(part, "zh", 0, 0, tiled=True)
    part = small(functools.partial(choose_kernel, 1), GROUPS, owner, part)
    own = lax.all_to_all(part, SPREAD, 0, 0, tiled=True)
    sib = lax.ppermute(own, "c", swap)
    return update(owner, own, sib, features, residual, coeffs, inverse, offsets)


def solution(mesh):
    fine = Mesh(mesh.devices.reshape(2, 4, 2, 4, 2, 2), AXES)
    cols = P(None, AXES)
    return jax.shard_map(
        shards,
        mesh=fine,
        in_specs=(cols, cols, cols, P(), P(), P()),
        out_specs=(cols, cols),
        check_vma=False,
    )
```

```python
import functools
import math

import jax
import jax.numpy as jnp
from jax import lax
from jax.experimental import pallas as pl
from jax.experimental.pallas import tpu as pltpu
from jax.sharding import Mesh, PartitionSpec as P

STEPS = 2
F, C, B, R = 440, 147, 512, 4096
FP, CP = 448, 160
ROWS = 768
HALF = 256
GROUPS = 32
PIECE = 48
KT = 1024
TILE = 1024
AXES = ("yl", "zh", "zl", "x", "c", "yh")
SPREAD = ("yl", "zl", "x", "yh")
BF, F32 = jnp.bfloat16, jnp.float32
HIGH = lax.Precision.HIGHEST


def split(value, terms):
    parts = []
    for _ in range(terms):
        part = value.astype(BF)
        parts.append(part)
        value = value - part.astype(F32)
    return parts


def dot(a, b):
    return jnp.dot(a, b, preferred_element_type=F32)


def norm_rows(wide, first):
    terms = split(-0.5 * jnp.sum(wide * wide, axis=0, keepdims=True), 3)
    norms = [part.astype(F32) for part in terms]
    ones = [jnp.ones((3, wide.shape[1]), F32)]
    rest = [jnp.zeros((2, wide.shape[1]), F32)]
    return jnp.concatenate((norms + ones if first else ones + norms) + rest, axis=0).astype(BF)


def whole_vmem():
    return pl.BlockSpec(memory_space=pltpu.VMEM)


def in_hbm():
    return pl.BlockSpec(memory_space=pltpu.HBM)


def stay(*arrays):
    return [pltpu.with_memory_space_constraint(a, pltpu.HBM) for a in arrays]


def in_smem():
    return pl.BlockSpec(memory_space=pltpu.SMEM)


def parts_of(owner):
    group = ((owner // 128 * 2 + owner // 16 % 2) * 4 + owner // 4 % 4) * 2 + owner % 2
    return group, owner // 32 % 4, owner // 2 % 2


def pick_kernel(owner, feat, res, inv, offs, own, sib, vfeat, vres, vinv, voffs, left, acc, msg, sems):
    me = lax.axis_index(AXES)
    core = lax.axis_index("c")
    chunks = R // KT

    def cols(i):
        return pl.ds(pl.multiple_of(i * KT, KT), KT)

    def one_step(step, carry):
        load_offs = pltpu.make_async_copy(offs, voffs, sems.at[2 * chunks])
        load_inv = pltpu.make_async_copy(inv.at[step], vinv, sems.at[2 * chunks + 1])

        def load_feat(i):
            return pltpu.make_async_copy(feat.at[:, cols(i)], vfeat.at[:, cols(i)], sems.at[2 * i])

        def load_res(i):
            return pltpu.make_async_copy(res.at[:, cols(i)], vres.at[:, cols(i)], sems.at[2 * i + 1])

        def chunk(i, carry):
            load_feat(i).wait()
            load_res(i).wait()
            left[:F, :] = vfeat[:, cols(i)]
            for k, part in enumerate(split(vres[:, cols(i)], 3)):
                left[FP + k * CP : FP + k * CP + C, :] = part
            row = lax.broadcasted_iota(jnp.int32, (KT, B), 0) + i * KT
            hot = jnp.where(row == voffs[pl.ds(step, 1), :], 1.0, 0.0).astype(BF)
            acc[...] += dot(left[...], hot)
            return carry

        @pl.when(owner[step] == me)
        def _():
            load_offs.start()
            for i in range(chunks):
                load_feat(i).start()
                load_res(i).start()
            load_inv.start()
            acc[...] = jnp.zeros_like(acc)
            load_offs.wait()
            lax.fori_loop(0, chunks, chunk, 0)
            block = acc[:F, :]
            msg[:F, :] = block.astype(BF)
            msg[F:FP, :] = norm_rows(block, True)
            found = acc[FP : FP + C, :] + (
                acc[FP + CP : FP + CP + C, :] + acc[FP + 2 * CP : FP + 2 * CP + C, :]
            )
            load_inv.wait()
            prod = jnp.dot(found, vinv[...], precision=HIGH, preferred_element_type=F32)
            for k, part in enumerate(split(prod, 2)):
                msg[FP + k * CP : FP + k * CP + C, :] = part
            rows = pl.ds(pl.multiple_of(PIECE * step, PIECE), PIECE)
            for out, half in ((own, core), (sib, 1 - core)):
                for cb in range(2):
                    lanes = pl.ds(pl.multiple_of(half * HALF + cb * 128, 128), 128)
                    for rg in range(16):
                        out[cb * 16 + rg, rows, :] = msg[rg * PIECE : (rg + 1) * PIECE, lanes]

        return carry

    lax.fori_loop(0, STEPS, one_step, 0)


def pick(owner, features, residual, inverse, offsets):
    piece = pltpu.VMEM((GROUPS, 2 * PIECE, 128), BF)
    return pl.pallas_call(
        pick_kernel,
        in_specs=[in_smem()] + [in_hbm()] * 4,
        out_specs=[whole_vmem()] * 2,
        scratch_shapes=[
            pltpu.VMEM((F, R), BF),
            pltpu.VMEM((C, R), F32),
            pltpu.VMEM((B, B), F32),
            pltpu.VMEM((STEPS, B), jnp.int32),
            pltpu.VMEM((FP + 3 * CP, KT), BF),
            pltpu.VMEM((FP + 3 * CP, B), F32),
            pltpu.VMEM((ROWS, B), BF),
            pltpu.SemaphoreType.DMA((2 * (R // KT) + 2,)),
        ],
        out_shape=[piece, piece],
        compiler_params=pltpu.CompilerParams(vmem_limit_bytes=20 * 1024 * 1024),
        name="pick",
    )(owner, *stay(features, residual, inverse, offsets))


def half_kernel(owner, own, got, out):
    core = lax.axis_index("c")
    for step in range(STEPS):
        rows = slice(PIECE * step, PIECE * (step + 1))
        here = owner[step] // 2 % 2 == core

        @pl.when(here)
        def _():
            out[:, rows, :] = own[:, rows, :]

        @pl.when(jnp.logical_not(here))
        def _():
            out[:, rows, :] = got[:, rows, :]


def choose_kernel(which, owner, stack, out):
    for step in range(STEPS):
        rows = slice(PIECE * step, PIECE * (step + 1))
        piece = stack[parts_of(owner[step])[which], rows, :]
        for i in range(out.shape[0]):
            out[i, rows, :] = piece


def small(kernel, count, owner, *arrays):
    return pl.pallas_call(
        kernel,
        in_specs=[in_smem()] + [whole_vmem()] * len(arrays),
        out_specs=whole_vmem(),
        out_shape=jax.ShapeDtypeStruct((count, 2 * PIECE, 128), BF),
        compiler_params=pltpu.CompilerParams(vmem_limit_bytes=4 * 1024 * 1024),
        name="choose",
    )(owner, *arrays)


def kernel_of(lhs, rhs):
    return jnp.exp2(dot(lhs, rhs) * (4.0 * math.log2(math.e) / F)).astype(BF)


def unpack(src, blk, blkt):
    for step in range(STEPS):
        for cb in range(2):
            lanes = slice(cb * 128, (cb + 1) * 128)
            for rg in range(16):
                blk[step, rg * PIECE : (rg + 1) * PIECE, lanes] = src[
                    cb * 16 + rg, PIECE * step : PIECE * (step + 1), :
                ]
        blkt[step] = blk[step, :FP, :].astype(F32).T.astype(BF)


def early_kernel(own, feat, res, wide, part, blk, blkt, vfeat, vres, sems):
    tiles = R // TILE

    def cols(i):
        return pl.ds(pl.multiple_of(i * TILE, TILE), TILE)

    def load_feat(i):
        return pltpu.make_async_copy(feat.at[:, cols(i)], vfeat.at[:, cols(i)], sems.at[i])

    def load_res(i):
        return pltpu.make_async_copy(res.at[:, cols(i)], vres.at[:, cols(i)], sems.at[tiles + i])

    for i in range(tiles):
        load_feat(i).start()
        load_res(i).start()
    unpack(own, blk, blkt)

    def body(i, carry):
        load_feat(i).wait()
        tile = vfeat[:, cols(i)]
        wide[:F, cols(i)] = tile
        wide[F:, cols(i)] = norm_rows(tile.astype(F32), False)
        change = dot(blk[0, FP : FP + C, :], kernel_of(blkt[0], wide[:, cols(i)]))
        load_res(i).wait()
        part[:, cols(i)] = vres[:, cols(i)] - change
        return carry

    lax.fori_loop(0, tiles, body, 0)


def early(own, features, residual):
    tiles = R // TILE
    return pl.pallas_call(
        early_kernel,
        in_specs=[whole_vmem()] + [in_hbm()] * 2,
        out_specs=[whole_vmem()] * 4,
        scratch_shapes=[
            pltpu.VMEM((F, R), BF),
            pltpu.VMEM((C, R), F32),
            pltpu.SemaphoreType.DMA((2 * tiles,)),
        ],
        out_shape=[
            pltpu.VMEM((FP, R), BF),
            pltpu.VMEM((C, R), F32),
            pltpu.VMEM((STEPS, ROWS, HALF), BF),
            pltpu.VMEM((STEPS, HALF, FP), BF),
        ],
        compiler_params=pltpu.CompilerParams(vmem_limit_bytes=12 * 1024 * 1024),
        name="early",
    )(own, *stay(features, residual))


def update_kernel(
    owner, sib, wide, part, blk0, blkt0, coef, inv, offs, new_res, new_coef,
    vres, vcoef, vinv, voffs, vcol, blk, blkt, right, left, delta, extra, sems, out_sems,
):
    me = lax.axis_index(AXES)
    mine = lax.axis_index("c")
    tiles = R // TILE
    holds = [owner[step] == me for step in range(STEPS)]
    either = holds[0] | holds[1]
    same_owner = owner[0] == owner[1]

    def cols(i):
        return pl.ds(pl.multiple_of(i * TILE, TILE), TILE)

    def half(i):
        return pl.ds(pl.multiple_of((mine if i == 0 else 1 - mine) * HALF, HALF), HALF)

    def here(i):
        return slice(i * HALF, (i + 1) * HALF)

    def store_res(i):
        return pltpu.make_async_copy(vres.at[:, cols(i)], new_res.at[:, cols(i)], out_sems.at[i])

    def store_coef(i):
        return pltpu.make_async_copy(vcoef.at[:, cols(i)], new_coef.at[:, cols(i)], out_sems.at[tiles + i])

    load_coef = pltpu.make_async_copy(coef, vcoef, sems.at[0])
    load_inv = [
        pltpu.make_async_copy(inv.at[1, half(i), half(j)], vinv.at[here(i), here(j)], sems.at[1 + 2 * i + j])
        for i in range(2)
        for j in range(2)
    ]
    load_offs = [pltpu.make_async_copy(offs.at[:, half(j)], voffs.at[:, here(j)], sems.at[5 + j]) for j in range(2)]
    for copy in load_inv + load_offs + [load_coef]:
        copy.start()
    unpack(sib, blk, blkt)
    left[:HALF, :] = blkt[0]
    left[HALF : 2 * HALF, :] = blkt0[1]
    left[2 * HALF :, :] = blkt[1]
    right[:F, :HALF] = blk0[1, :F, :]
    right[:F, HALF:] = blk[1, :F, :]
    right[F:, :] = norm_rows(right[:F, :].astype(F32), False)
    first = blk0[0, FP : FP + C, :]
    second = blk[0, FP : FP + C, :]
    delta[:, :HALF] = second
    extra[...] = dot(first, kernel_of(blkt0[0], right[...])) + dot(second, kernel_of(blkt[0], right[...]))
    for copy in load_offs:
        copy.wait()

    @pl.when(either | same_owner)
    def _():
        vcol[...] = jnp.concatenate([voffs[...]] * 4, axis=0).T

    @pl.when(same_owner)
    def _():
        meet = jnp.where(vcol[:, 0:1] == voffs[1:2, :], 0.5, 0.0).astype(BF)
        extra[...] += dot(first, meet[:HALF, :]) + dot(second, meet[HALF:, :])

    for copy in load_inv:
        copy.wait()
    lost = jnp.dot(extra[...], vinv[...], precision=HIGH, preferred_element_type=F32)
    for i, src in enumerate((blk0, blk)):
        base = src[1, FP : FP + C, :].astype(F32) + src[1, FP + CP : FP + CP + C, :].astype(F32)
        delta[:, (i + 1) * HALF : (i + 2) * HALF] = (base - lost[:, here(i)]).astype(BF)
    load_coef.wait()

    @pl.when(jnp.logical_not(either))
    def _():
        for i in range(tiles):
            store_coef(i).start()

    def body(i, carry):
        vres[:, cols(i)] = part[:, cols(i)] - dot(delta[...], kernel_of(left[...], wide[:, cols(i)]))

        @pl.when(either)
        def _():
            for step in range(STEPS):

                @pl.when(holds[step])
                def _():
                    col = lax.broadcasted_iota(jnp.int32, (B, TILE), 1) + i * TILE
                    hot = jnp.where(col == vcol[:, step : step + 1], 1.0, 0.0).astype(BF)
                    if step == 0:
                        placed = dot(first, hot[:HALF, :]) + dot(second, hot[HALF:, :])
                    else:
                        placed = dot(delta[:, HALF:], hot)
                    vres[:, cols(i)] -= 0.5 * placed
                    vcoef[:, cols(i)] += placed

            store_coef(i).start()

        store_res(i).start()
        return carry

    lax.fori_loop(0, tiles, body, 0)
    for i in range(tiles):
        store_res(i).wait()
        store_coef(i).wait()


def update(owner, sib, wide, part, blk, blkt, coeffs, inverse, offsets):
    out = jax.ShapeDtypeStruct((C, R), F32)
    tiles = R // TILE
    near = [pltpu.with_memory_space_constraint(a, pltpu.VMEM) for a in (sib, wide, part, blk, blkt)]
    return pl.pallas_call(
        update_kernel,
        in_specs=[in_smem()] + [whole_vmem()] * 5 + [in_hbm()] * 3,
        out_specs=[in_hbm()] * 2,
        scratch_shapes=[
            pltpu.VMEM((C, R), F32),
            pltpu.VMEM((C, R), F32),
            pltpu.VMEM((B, B), F32),
            pltpu.VMEM((STEPS, B), jnp.int32),
            pltpu.VMEM((B, 8), jnp.int32),
            pltpu.VMEM((STEPS, ROWS, HALF), BF),
            pltpu.VMEM((STEPS, HALF, FP), BF),
            pltpu.VMEM((FP, B), BF),
            pltpu.VMEM((3 * HALF, FP), BF),
            pltpu.VMEM((C, 3 * HALF), BF),
            pltpu.VMEM((C, B), F32),
            pltpu.SemaphoreType.DMA((7,)),
            pltpu.SemaphoreType.DMA((2 * tiles,)),
        ],
        out_shape=[out, out],
        compiler_params=pltpu.CompilerParams(vmem_limit_bytes=24 * 1024 * 1024),
        name="update",
    )(owner, *near, *stay(coeffs, inverse, offsets))


def shards(features, residual, coeffs, inverse, owner, offsets):
    swap = [(0, 1), (1, 0)]
    (owner,) = stay(owner)
    own, sib = pick(owner, features, residual, inverse, offsets)
    half = small(half_kernel, GROUPS, owner, own, lax.ppermute(sib, "c", swap))
    part = lax.all_to_all(half, SPREAD, 0, 0, tiled=True)
    part = small(functools.partial(choose_kernel, 0), 4, owner, part)
    part = lax.all_to_all(part, "zh", 0, 0, tiled=True)
    part = small(functools.partial(choose_kernel, 1), GROUPS, owner, part)
    own = lax.all_to_all(part, SPREAD, 0, 0, tiled=True)
    sib = lax.ppermute(own, "c", swap)
    held = early(own, features, residual)
    return update(owner, sib, *held, coeffs, inverse, offsets)


def solution(mesh):
    fine = Mesh(mesh.devices.reshape(2, 4, 2, 4, 2, 2), AXES)
    cols = P(None, AXES)
    return jax.shard_map(
        shards,
        mesh=fine,
        in_specs=(cols, cols, cols, P(), P(), P()),
        out_specs=(cols, cols),
        check_vma=False,
    )
```

```python
import functools
import math

import jax
import jax.numpy as jnp
from jax import lax
from jax.experimental import pallas as pl
from jax.experimental.pallas import tpu as pltpu
from jax.sharding import Mesh, PartitionSpec as P

STEPS = 2
F, C, B, R = 440, 147, 512, 4096
FP, CP = 448, 160
ROWS = 768
HALF = 256
GROUPS = 32
PIECE = 48
KT = 1024
TILE = 1024
WIDE = 2048
AXES = ("yl", "zh", "zl", "x", "c", "yh")
SPREAD = ("yl", "zl", "x", "yh")
BF, F32 = jnp.bfloat16, jnp.float32
HIGH = lax.Precision.HIGHEST


def split(value, terms):
    parts = []
    for _ in range(terms):
        part = value.astype(BF)
        parts.append(part)
        value = value - part.astype(F32)
    return parts


def dot(a, b):
    return jnp.dot(a, b, preferred_element_type=F32)


def norm_rows(wide, first):
    terms = split(-0.5 * jnp.sum(wide * wide, axis=0, keepdims=True), 3)
    norms = [part.astype(F32) for part in terms]
    ones = [jnp.ones((3, wide.shape[1]), F32)]
    rest = [jnp.zeros((2, wide.shape[1]), F32)]
    return jnp.concatenate((norms + ones if first else ones + norms) + rest, axis=0).astype(BF)


def whole_vmem():
    return pl.BlockSpec(memory_space=pltpu.VMEM)


def in_hbm():
    return pl.BlockSpec(memory_space=pltpu.HBM)


def stay(*arrays):
    return [pltpu.with_memory_space_constraint(a, pltpu.HBM) for a in arrays]


def in_smem():
    return pl.BlockSpec(memory_space=pltpu.SMEM)


def parts_of(owner):
    group = ((owner // 128 * 2 + owner // 16 % 2) * 4 + owner // 4 % 4) * 2 + owner % 2
    return group, owner // 32 % 4, owner // 2 % 2


def pick_kernel(owner, feat, res, inv, offs, own, sib, vfeat, vres, vinv, voffs, left, acc, msg, sems):
    me = lax.axis_index(AXES)
    core = lax.axis_index("c")
    chunks = R // KT

    def cols(i):
        return pl.ds(pl.multiple_of(i * KT, KT), KT)

    def one_step(step, carry):
        load_offs = pltpu.make_async_copy(offs, voffs, sems.at[2 * chunks])
        load_inv = pltpu.make_async_copy(inv.at[step], vinv, sems.at[2 * chunks + 1])

        def load_feat(i):
            return pltpu.make_async_copy(feat.at[:, cols(i)], vfeat.at[:, cols(i)], sems.at[2 * i])

        def load_res(i):
            return pltpu.make_async_copy(res.at[:, cols(i)], vres.at[:, cols(i)], sems.at[2 * i + 1])

        def chunk(i):
            load_feat(i).wait()
            load_res(i).wait()
            left[i % 2, :F, :] = vfeat[:, cols(i)]
            for k, part in enumerate(split(vres[:, cols(i)], 3)):
                left[i % 2, FP + k * CP : FP + k * CP + C, :] = part
            row = lax.broadcasted_iota(jnp.int32, (KT, B), 0) + i * KT
            hot = jnp.where(row == voffs[pl.ds(step, 1), :], 1.0, 0.0).astype(BF)
            found = dot(left[i % 2], hot)
            acc[...] = found if i == 0 else acc[...] + found

        @pl.when(owner[step] == me)
        def _():
            load_offs.start()
            for i in range(chunks):
                load_feat(i).start()
                load_res(i).start()
            load_inv.start()
            load_offs.wait()
            for i in range(chunks):
                chunk(i)
            block = acc[:F, :]
            msg[:F, :] = block.astype(BF)
            msg[F:FP, :] = norm_rows(block, True)
            found = acc[FP : FP + C, :] + (
                acc[FP + CP : FP + CP + C, :] + acc[FP + 2 * CP : FP + 2 * CP + C, :]
            )
            load_inv.wait()
            prod = jnp.dot(found, vinv[...], precision=HIGH, preferred_element_type=F32)
            for k, part in enumerate(split(prod, 2)):
                msg[FP + k * CP : FP + k * CP + C, :] = part
            rows = pl.ds(pl.multiple_of(PIECE * step, PIECE), PIECE)
            for out, half in ((own, core), (sib, 1 - core)):
                for cb in range(2):
                    lanes = pl.ds(pl.multiple_of(half * HALF + cb * 128, 128), 128)
                    for rg in range(16):
                        out[cb * 16 + rg, rows, :] = msg[rg * PIECE : (rg + 1) * PIECE, lanes]

        return carry

    lax.fori_loop(0, STEPS, one_step, 0)


def pick(owner, features, residual, inverse, offsets):
    piece = pltpu.VMEM((GROUPS, 2 * PIECE, 128), BF)
    return pl.pallas_call(
        pick_kernel,
        in_specs=[in_smem()] + [in_hbm()] * 4,
        out_specs=[whole_vmem()] * 2,
        scratch_shapes=[
            pltpu.VMEM((F, R), BF),
            pltpu.VMEM((C, R), F32),
            pltpu.VMEM((B, B), F32),
            pltpu.VMEM((STEPS, B), jnp.int32),
            pltpu.VMEM((2, FP + 3 * CP, KT), BF),
            pltpu.VMEM((FP + 3 * CP, B), F32),
            pltpu.VMEM((ROWS, B), BF),
            pltpu.SemaphoreType.DMA((2 * (R // KT) + 2,)),
        ],
        out_shape=[piece, piece],
        compiler_params=pltpu.CompilerParams(vmem_limit_bytes=20 * 1024 * 1024),
        name="pick",
    )(owner, *stay(features, residual, inverse, offsets))


def half_kernel(owner, own, got, out):
    core = lax.axis_index("c")
    for step in range(STEPS):
        rows = slice(PIECE * step, PIECE * (step + 1))
        here = owner[step] // 2 % 2 == core

        @pl.when(here)
        def _():
            out[:, rows, :] = own[:, rows, :]

        @pl.when(jnp.logical_not(here))
        def _():
            out[:, rows, :] = got[:, rows, :]


def choose_kernel(which, owner, stack, out):
    for step in range(STEPS):
        rows = slice(PIECE * step, PIECE * (step + 1))
        piece = stack[parts_of(owner[step])[which], rows, :]
        for i in range(out.shape[0]):
            out[i, rows, :] = piece


def small(kernel, count, owner, *arrays):
    return pl.pallas_call(
        kernel,
        in_specs=[in_smem()] + [whole_vmem()] * len(arrays),
        out_specs=whole_vmem(),
        out_shape=jax.ShapeDtypeStruct((count, 2 * PIECE, 128), BF),
        compiler_params=pltpu.CompilerParams(vmem_limit_bytes=4 * 1024 * 1024),
        name="choose",
    )(owner, *arrays)


def kernel_of(lhs, rhs):
    return jnp.exp2(dot(lhs, rhs) * (4.0 * math.log2(math.e) / F)).astype(BF)


def unpack(src, blk, blkt):
    for step in range(STEPS):
        for cb in range(2):
            lanes = slice(cb * 128, (cb + 1) * 128)
            for rg in range(16):
                blk[step, rg * PIECE : (rg + 1) * PIECE, lanes] = src[
                    cb * 16 + rg, PIECE * step : PIECE * (step + 1), :
                ]
        blkt[step] = blk[step, :FP, :].astype(F32).T.astype(BF)


def early_kernel(own, feat, res, coef, wide, part, blk, blkt, vcoef, vfeat, vres, sems):
    tiles = R // WIDE

    def cols(i):
        return pl.ds(pl.multiple_of(i * WIDE, WIDE), WIDE)

    def load_feat(i):
        return pltpu.make_async_copy(feat.at[:, cols(i)], vfeat.at[:, cols(i)], sems.at[i])

    def load_res(i):
        return pltpu.make_async_copy(res.at[:, cols(i)], vres.at[:, cols(i)], sems.at[tiles + i])

    for i in range(tiles):
        load_feat(i).start()
        load_res(i).start()
    load_coef = pltpu.make_async_copy(coef, vcoef, sems.at[2 * tiles])
    load_coef.start()
    unpack(own, blk, blkt)

    def body(i, carry):
        load_feat(i).wait()
        tile = vfeat[:, cols(i)]
        wide[:F, cols(i)] = tile
        wide[F:, cols(i)] = norm_rows(tile.astype(F32), False)
        change = dot(blk[0, FP : FP + C, :], kernel_of(blkt[0], wide[:, cols(i)]))
        load_res(i).wait()
        part[:, cols(i)] = vres[:, cols(i)] - change
        return carry

    lax.fori_loop(0, tiles, body, 0)
    load_coef.wait()


def early(own, features, residual, coeffs):
    tiles = R // WIDE
    return pl.pallas_call(
        early_kernel,
        in_specs=[whole_vmem()] + [in_hbm()] * 3,
        out_specs=[whole_vmem()] * 5,
        scratch_shapes=[
            pltpu.VMEM((F, R), BF),
            pltpu.VMEM((C, R), F32),
            pltpu.SemaphoreType.DMA((2 * tiles + 1,)),
        ],
        out_shape=[
            pltpu.VMEM((FP, R), BF),
            pltpu.VMEM((C, R), F32),
            pltpu.VMEM((STEPS, ROWS, HALF), BF),
            pltpu.VMEM((STEPS, HALF, FP), BF),
            pltpu.VMEM((C, R), F32),
        ],
        compiler_params=pltpu.CompilerParams(vmem_limit_bytes=12 * 1024 * 1024),
        name="early",
    )(own, *stay(features, residual, coeffs))


def update_kernel(
    owner, sib, wide, part, blk0, blkt0, coef, inv, offs, new_res, new_coef,
    vres, vcoef, vinv, voffs, vcol, blk, blkt, right, left, delta, extra, sems, out_sems,
):
    me = lax.axis_index(AXES)
    mine = lax.axis_index("c")
    tiles = R // TILE
    holds = [owner[step] == me for step in range(STEPS)]
    either = holds[0] | holds[1]
    same_owner = owner[0] == owner[1]

    def cols(i):
        return pl.ds(pl.multiple_of(i * TILE, TILE), TILE)

    def half(i):
        return pl.ds(pl.multiple_of((mine if i == 0 else 1 - mine) * HALF, HALF), HALF)

    def here(i):
        return slice(i * HALF, (i + 1) * HALF)

    def store_res(i):
        return pltpu.make_async_copy(vres.at[:, cols(i)], new_res.at[:, cols(i)], out_sems.at[i])

    def store_coef(i):
        return pltpu.make_async_copy(vcoef.at[:, cols(i)], new_coef.at[:, cols(i)], out_sems.at[tiles + i])

    def store_same(i):
        return pltpu.make_async_copy(coef.at[:, cols(i)], new_coef.at[:, cols(i)], out_sems.at[tiles + i])

    load_inv = [
        pltpu.make_async_copy(inv.at[1, half(i), half(j)], vinv.at[here(i), here(j)], sems.at[1 + 2 * i + j])
        for i in range(2)
        for j in range(2)
    ]
    load_offs = [pltpu.make_async_copy(offs.at[:, half(j)], voffs.at[:, here(j)], sems.at[5 + j]) for j in range(2)]
    for copy in load_inv + load_offs:
        copy.start()

    @pl.when(jnp.logical_not(either))
    def _():
        for i in range(tiles):
            store_same(i).start()

    unpack(sib, blk, blkt)
    left[:HALF, :] = blkt[0]
    left[HALF : 2 * HALF, :] = blkt0[1]
    left[2 * HALF :, :] = blkt[1]
    right[:F, :HALF] = blk0[1, :F, :]
    right[:F, HALF:] = blk[1, :F, :]
    right[F:, :] = norm_rows(right[:F, :].astype(F32), False)
    first = blk0[0, FP : FP + C, :]
    second = blk[0, FP : FP + C, :]
    delta[:, :HALF] = second
    extra[...] = dot(first, kernel_of(blkt0[0], right[...])) + dot(second, kernel_of(blkt[0], right[...]))
    for copy in load_offs:
        copy.wait()

    @pl.when(either | same_owner)
    def _():
        vcol[...] = jnp.concatenate([voffs[...]] * 4, axis=0).T

    @pl.when(same_owner)
    def _():
        meet = jnp.where(vcol[:, 0:1] == voffs[1:2, :], 0.5, 0.0).astype(BF)
        extra[...] += dot(first, meet[:HALF, :]) + dot(second, meet[HALF:, :])

    for copy in load_inv:
        copy.wait()
    top, low = split(extra[...], 2)
    major, minor = split(vinv[...], 2)
    lost = dot(top, major) + (dot(low, major) + dot(top, minor))
    for i, src in enumerate((blk0, blk)):
        base = src[1, FP : FP + C, :].astype(F32) + src[1, FP + CP : FP + CP + C, :].astype(F32)
        delta[:, (i + 1) * HALF : (i + 2) * HALF] = (base - lost[:, here(i)]).astype(BF)

    def body(i, carry):
        vres[:, cols(i)] = part[:, cols(i)] - dot(delta[...], kernel_of(left[...], wide[:, cols(i)]))

        @pl.when(either)
        def _():
            vcoef[:, cols(i)] = coef[:, cols(i)]
            for step in range(STEPS):

                @pl.when(holds[step])
                def _():
                    col = lax.broadcasted_iota(jnp.int32, (B, TILE), 1) + i * TILE
                    hot = jnp.where(col == vcol[:, step : step + 1], 1.0, 0.0).astype(BF)
                    if step == 0:
                        placed = dot(first, hot[:HALF, :]) + dot(second, hot[HALF:, :])
                    else:
                        placed = dot(delta[:, HALF:], hot)
                    vres[:, cols(i)] -= 0.5 * placed
                    vcoef[:, cols(i)] += placed

            store_coef(i).start()

        store_res(i).start()
        return carry

    lax.fori_loop(0, tiles, body, 0)
    for i in range(tiles):
        store_res(i).wait()
        store_coef(i).wait()


def update(owner, sib, wide, part, blk, blkt, coef, inverse, offsets):
    out = jax.ShapeDtypeStruct((C, R), F32)
    tiles = R // TILE
    near = [pltpu.with_memory_space_constraint(a, pltpu.VMEM) for a in (sib, wide, part, blk, blkt, coef)]
    return pl.pallas_call(
        update_kernel,
        in_specs=[in_smem()] + [whole_vmem()] * 6 + [in_hbm()] * 2,
        out_specs=[in_hbm()] * 2,
        scratch_shapes=[
            pltpu.VMEM((C, R), F32),
            pltpu.VMEM((C, R), F32),
            pltpu.VMEM((B, B), F32),
            pltpu.VMEM((STEPS, B), jnp.int32),
            pltpu.VMEM((B, 8), jnp.int32),
            pltpu.VMEM((STEPS, ROWS, HALF), BF),
            pltpu.VMEM((STEPS, HALF, FP), BF),
            pltpu.VMEM((FP, B), BF),
            pltpu.VMEM((3 * HALF, FP), BF),
            pltpu.VMEM((C, 3 * HALF), BF),
            pltpu.VMEM((C, B), F32),
            pltpu.SemaphoreType.DMA((7,)),
            pltpu.SemaphoreType.DMA((2 * tiles,)),
        ],
        out_shape=[out, out],
        compiler_params=pltpu.CompilerParams(vmem_limit_bytes=24 * 1024 * 1024),
        name="update",
    )(owner, *near, *stay(inverse, offsets))


def shards(features, residual, coeffs, inverse, owner, offsets):
    swap = [(0, 1), (1, 0)]
    (owner,) = stay(owner)
    own, sib = pick(owner, features, residual, inverse, offsets)
    half = small(half_kernel, GROUPS, owner, own, lax.ppermute(sib, "c", swap))
    part = lax.all_to_all(half, SPREAD, 0, 0, tiled=True)
    part = small(functools.partial(choose_kernel, 0), 4, owner, part)
    part = lax.all_to_all(part, "zh", 0, 0, tiled=True)
    part = small(functools.partial(choose_kernel, 1), GROUPS, owner, part)
    own = lax.all_to_all(part, SPREAD, 0, 0, tiled=True)
    sib = lax.ppermute(own, "c", swap)
    held = early(own, features, residual, coeffs)
    return update(owner, sib, *held, inverse, offsets)


def solution(mesh):
    fine = Mesh(mesh.devices.reshape(2, 4, 2, 4, 2, 2), AXES)
    cols = P(None, AXES)
    return jax.shard_map(
        shards,
        mesh=fine,
        in_specs=(cols, cols, cols, P(), P(), P()),
        out_specs=(cols, cols),
        check_vma=False,
    )
```

```python
import functools
import math

import jax
import jax.numpy as jnp
from jax import lax
from jax.experimental import pallas as pl
from jax.experimental.pallas import tpu as pltpu
from jax.sharding import Mesh, PartitionSpec as P

STEPS = 2
F, C, B, R = 440, 147, 512, 4096
FP, CP = 448, 160
ROWS = 768
HALF = 256
GROUPS = 32
PIECE = 48
KT = 1024
TILE = 1024
WIDE = 2048
AXES = ("yl", "zh", "zl", "x", "c", "yh")
SPREAD = ("yl", "zl", "x", "yh")
BF, F32 = jnp.bfloat16, jnp.float32
HIGH = lax.Precision.HIGHEST


def split(value, terms):
    parts = []
    for _ in range(terms):
        part = value.astype(BF)
        parts.append(part)
        value = value - part.astype(F32)
    return parts


def dot(a, b):
    return jnp.dot(a, b, preferred_element_type=F32)


def norm_rows(wide, first):
    terms = split(-0.5 * jnp.sum(wide * wide, axis=0, keepdims=True), 3)
    norms = [part.astype(F32) for part in terms]
    ones = [jnp.ones((3, wide.shape[1]), F32)]
    rest = [jnp.zeros((2, wide.shape[1]), F32)]
    return jnp.concatenate((norms + ones if first else ones + norms) + rest, axis=0).astype(BF)


def whole_vmem():
    return pl.BlockSpec(memory_space=pltpu.VMEM)


def in_hbm():
    return pl.BlockSpec(memory_space=pltpu.HBM)


def stay(*arrays):
    return [pltpu.with_memory_space_constraint(a, pltpu.HBM) for a in arrays]


def in_smem():
    return pl.BlockSpec(memory_space=pltpu.SMEM)


def parts_of(owner):
    group = ((owner // 128 * 2 + owner // 16 % 2) * 4 + owner // 4 % 4) * 2 + owner % 2
    return group, owner // 32 % 4, owner // 2 % 2


def pick_kernel(owner, feat, res, inv, offs, own, sib, known, vfeat, vres, vinv, voffs, left, acc, msg, sems):
    me = lax.axis_index(AXES)
    core = lax.axis_index("c")
    chunks = R // KT
    for step in range(STEPS):
        known[step] = owner[step]

    def cols(i):
        return pl.ds(pl.multiple_of(i * KT, KT), KT)

    def one_step(step, carry):
        load_offs = pltpu.make_async_copy(offs, voffs, sems.at[2 * chunks])
        load_inv = pltpu.make_async_copy(inv.at[step], vinv, sems.at[2 * chunks + 1])

        def load_feat(i):
            return pltpu.make_async_copy(feat.at[:, cols(i)], vfeat.at[:, cols(i)], sems.at[2 * i])

        def load_res(i):
            return pltpu.make_async_copy(res.at[:, cols(i)], vres.at[:, cols(i)], sems.at[2 * i + 1])

        def chunk(i):
            load_feat(i).wait()
            load_res(i).wait()
            left[i % 2, :F, :] = vfeat[:, cols(i)]
            for k, part in enumerate(split(vres[:, cols(i)], 3)):
                left[i % 2, FP + k * CP : FP + k * CP + C, :] = part
            row = lax.broadcasted_iota(jnp.int32, (KT, B), 0) + i * KT
            hot = jnp.where(row == voffs[pl.ds(step, 1), :], 1.0, 0.0).astype(BF)
            found = dot(left[i % 2], hot)
            acc[...] = found if i == 0 else acc[...] + found

        @pl.when(owner[step] == me)
        def _():
            load_offs.start()
            for i in range(chunks):
                load_feat(i).start()
                load_res(i).start()
            load_inv.start()
            load_offs.wait()
            for i in range(chunks):
                chunk(i)
            block = acc[:F, :]
            msg[:F, :] = block.astype(BF)
            msg[F:FP, :] = norm_rows(block, True)
            found = acc[FP : FP + C, :] + (
                acc[FP + CP : FP + CP + C, :] + acc[FP + 2 * CP : FP + 2 * CP + C, :]
            )
            load_inv.wait()
            prod = jnp.dot(found, vinv[...], precision=HIGH, preferred_element_type=F32)
            for k, part in enumerate(split(prod, 2)):
                msg[FP + k * CP : FP + k * CP + C, :] = part
            rows = pl.ds(pl.multiple_of(PIECE * step, PIECE), PIECE)
            for out, half in ((own, core), (sib, 1 - core)):
                for cb in range(2):
                    lanes = pl.ds(pl.multiple_of(half * HALF + cb * 128, 128), 128)
                    for rg in range(16):
                        out[cb * 16 + rg, rows, :] = msg[rg * PIECE : (rg + 1) * PIECE, lanes]

        return carry

    lax.fori_loop(0, STEPS, one_step, 0)


def pick(owner, features, residual, inverse, offsets):
    piece = pltpu.VMEM((GROUPS, 2 * PIECE, 128), BF)
    return pl.pallas_call(
        pick_kernel,
        in_specs=[in_smem()] + [in_hbm()] * 4,
        out_specs=[whole_vmem()] * 2 + [in_smem()],
        scratch_shapes=[
            pltpu.VMEM((F, R), BF),
            pltpu.VMEM((C, R), F32),
            pltpu.VMEM((B, B), F32),
            pltpu.VMEM((STEPS, B), jnp.int32),
            pltpu.VMEM((2, FP + 3 * CP, KT), BF),
            pltpu.VMEM((FP + 3 * CP, B), F32),
            pltpu.VMEM((ROWS, B), BF),
            pltpu.SemaphoreType.DMA((2 * (R // KT) + 2,)),
        ],
        out_shape=[piece, piece, pltpu.SMEM((STEPS,), jnp.int32)],
        compiler_params=pltpu.CompilerParams(vmem_limit_bytes=20 * 1024 * 1024),
        name="pick",
    )(owner, *stay(features, residual, inverse, offsets))


def half_kernel(owner, own, got, out):
    core = lax.axis_index("c")
    for step in range(STEPS):
        rows = slice(PIECE * step, PIECE * (step + 1))
        here = owner[step] // 2 % 2 == core

        @pl.when(here)
        def _():
            out[:, rows, :] = own[:, rows, :]

        @pl.when(jnp.logical_not(here))
        def _():
            out[:, rows, :] = got[:, rows, :]


def choose_kernel(which, owner, stack, out):
    for step in range(STEPS):
        rows = slice(PIECE * step, PIECE * (step + 1))
        piece = stack[parts_of(owner[step])[which], rows, :]
        for i in range(out.shape[0]):
            out[i, rows, :] = piece


def small(kernel, count, owner, *arrays):
    return pl.pallas_call(
        kernel,
        in_specs=[in_smem()] + [whole_vmem()] * len(arrays),
        out_specs=whole_vmem(),
        out_shape=jax.ShapeDtypeStruct((count, 2 * PIECE, 128), BF),
        compiler_params=pltpu.CompilerParams(vmem_limit_bytes=4 * 1024 * 1024),
        name="choose",
    )(owner, *arrays)


def kernel_of(lhs, rhs):
    return jnp.exp2(dot(lhs, rhs) * (4.0 * math.log2(math.e) / F)).astype(BF)


def unpack(src, blk, blkt):
    for step in range(STEPS):
        for cb in range(2):
            lanes = slice(cb * 128, (cb + 1) * 128)
            for rg in range(16):
                blk[step, rg * PIECE : (rg + 1) * PIECE, lanes] = src[
                    cb * 16 + rg, PIECE * step : PIECE * (step + 1), :
                ]
        blkt[step] = blk[step, :FP, :].astype(F32).T.astype(BF)


def early_kernel(own, feat, res, coef, wide, part, blk, blkt, vcoef, vfeat, vres, sems):
    tiles = R // WIDE

    def cols(i):
        return pl.ds(pl.multiple_of(i * WIDE, WIDE), WIDE)

    def load_feat(i):
        return pltpu.make_async_copy(feat.at[:, cols(i)], vfeat.at[:, cols(i)], sems.at[i])

    def load_res(i):
        return pltpu.make_async_copy(res.at[:, cols(i)], vres.at[:, cols(i)], sems.at[tiles + i])

    for i in range(tiles):
        load_feat(i).start()
        load_res(i).start()
    load_coef = pltpu.make_async_copy(coef, vcoef, sems.at[2 * tiles])
    load_coef.start()
    unpack(own, blk, blkt)

    def body(i, carry):
        load_feat(i).wait()
        tile = vfeat[:, cols(i)]
        wide[:F, cols(i)] = tile
        wide[F:, cols(i)] = norm_rows(tile.astype(F32), False)
        change = dot(blk[0, FP : FP + C, :], kernel_of(blkt[0], wide[:, cols(i)]))
        load_res(i).wait()
        part[:, cols(i)] = vres[:, cols(i)] - change
        return carry

    lax.fori_loop(0, tiles, body, 0)
    load_coef.wait()


def early(own, features, residual, coeffs):
    tiles = R // WIDE
    return pl.pallas_call(
        early_kernel,
        in_specs=[whole_vmem()] + [in_hbm()] * 3,
        out_specs=[whole_vmem()] * 5,
        scratch_shapes=[
            pltpu.VMEM((F, R), BF),
            pltpu.VMEM((C, R), F32),
            pltpu.SemaphoreType.DMA((2 * tiles + 1,)),
        ],
        out_shape=[
            pltpu.VMEM((FP, R), BF),
            pltpu.VMEM((C, R), F32),
            pltpu.VMEM((STEPS, ROWS, HALF), BF),
            pltpu.VMEM((STEPS, HALF, FP), BF),
            pltpu.VMEM((C, R), F32),
        ],
        compiler_params=pltpu.CompilerParams(vmem_limit_bytes=12 * 1024 * 1024),
        name="early",
    )(own, *stay(features, residual, coeffs))


def update_kernel(
    owner, sib, wide, part, blk0, blkt0, coef, inv, offs, new_res, new_coef,
    vres, vcoef, vinv, voffs, vcol, blk, blkt, right, left, delta, extra, sems, out_sems,
):
    me = lax.axis_index(AXES)
    mine = lax.axis_index("c")
    tiles = R // TILE
    holds = [owner[step] == me for step in range(STEPS)]
    either = holds[0] | holds[1]
    same_owner = owner[0] == owner[1]

    def cols(i):
        return pl.ds(pl.multiple_of(i * TILE, TILE), TILE)

    def half(i):
        return pl.ds(pl.multiple_of((mine if i == 0 else 1 - mine) * HALF, HALF), HALF)

    def here(i):
        return slice(i * HALF, (i + 1) * HALF)

    def store_res(i):
        return pltpu.make_async_copy(vres.at[:, cols(i)], new_res.at[:, cols(i)], out_sems.at[i])

    def store_coef(i):
        return pltpu.make_async_copy(vcoef.at[:, cols(i)], new_coef.at[:, cols(i)], out_sems.at[tiles + i])

    def store_same(i):
        return pltpu.make_async_copy(coef.at[:, cols(i)], new_coef.at[:, cols(i)], out_sems.at[tiles + i])

    load_inv = [
        pltpu.make_async_copy(inv.at[1, half(i), half(j)], vinv.at[here(i), here(j)], sems.at[1 + 2 * i + j])
        for i in range(2)
        for j in range(2)
    ]
    load_offs = [pltpu.make_async_copy(offs.at[:, half(j)], voffs.at[:, here(j)], sems.at[5 + j]) for j in range(2)]
    for copy in load_inv + load_offs:
        copy.start()

    @pl.when(jnp.logical_not(either))
    def _():
        for i in range(tiles):
            store_same(i).start()

    unpack(sib, blk, blkt)
    left[:HALF, :] = blkt[0]
    left[HALF : 2 * HALF, :] = blkt0[1]
    left[2 * HALF :, :] = blkt[1]
    right[:F, :HALF] = blk0[1, :F, :]
    right[:F, HALF:] = blk[1, :F, :]
    right[F:, :] = norm_rows(right[:F, :].astype(F32), False)
    first = blk0[0, FP : FP + C, :]
    second = blk[0, FP : FP + C, :]
    delta[:, :HALF] = second
    extra[...] = dot(first, kernel_of(blkt0[0], right[...])) + dot(second, kernel_of(blkt[0], right[...]))
    for copy in load_offs:
        copy.wait()

    @pl.when(either | same_owner)
    def _():
        vcol[...] = jnp.concatenate([voffs[...]] * 4, axis=0).T

    @pl.when(same_owner)
    def _():
        meet = jnp.where(vcol[:, 0:1] == voffs[1:2, :], 0.5, 0.0).astype(BF)
        extra[...] += dot(first, meet[:HALF, :]) + dot(second, meet[HALF:, :])

    for copy in load_inv:
        copy.wait()
    top, low = split(extra[...], 2)
    major, minor = split(vinv[...], 2)
    lost = dot(top, major) + (dot(low, major) + dot(top, minor))
    for i, src in enumerate((blk0, blk)):
        base = src[1, FP : FP + C, :].astype(F32) + src[1, FP + CP : FP + CP + C, :].astype(F32)
        delta[:, (i + 1) * HALF : (i + 2) * HALF] = (base - lost[:, here(i)]).astype(BF)

    def body(i, carry):
        vres[:, cols(i)] = part[:, cols(i)] - dot(delta[...], kernel_of(left[...], wide[:, cols(i)]))

        @pl.when(either)
        def _():
            vcoef[:, cols(i)] = coef[:, cols(i)]
            for step in range(STEPS):

                @pl.when(holds[step])
                def _():
                    col = lax.broadcasted_iota(jnp.int32, (B, TILE), 1) + i * TILE
                    hot = jnp.where(col == vcol[:, step : step + 1], 1.0, 0.0).astype(BF)
                    if step == 0:
                        placed = dot(first, hot[:HALF, :]) + dot(second, hot[HALF:, :])
                    else:
                        placed = dot(delta[:, HALF:], hot)
                    vres[:, cols(i)] -= 0.5 * placed
                    vcoef[:, cols(i)] += placed

            store_coef(i).start()

        store_res(i).start()
        return carry

    lax.fori_loop(0, tiles, body, 0)
    for i in range(tiles):
        store_res(i).wait()
        store_coef(i).wait()


def update(owner, sib, wide, part, blk, blkt, coef, inverse, offsets):
    out = jax.ShapeDtypeStruct((C, R), F32)
    tiles = R // TILE
    near = [pltpu.with_memory_space_constraint(a, pltpu.VMEM) for a in (sib, wide, part, blk, blkt, coef)]
    return pl.pallas_call(
        update_kernel,
        in_specs=[in_smem()] + [whole_vmem()] * 6 + [in_hbm()] * 2,
        out_specs=[in_hbm()] * 2,
        scratch_shapes=[
            pltpu.VMEM((C, R), F32),
            pltpu.VMEM((C, R), F32),
            pltpu.VMEM((B, B), F32),
            pltpu.VMEM((STEPS, B), jnp.int32),
            pltpu.VMEM((B, 8), jnp.int32),
            pltpu.VMEM((STEPS, ROWS, HALF), BF),
            pltpu.VMEM((STEPS, HALF, FP), BF),
            pltpu.VMEM((FP, B), BF),
            pltpu.VMEM((3 * HALF, FP), BF),
            pltpu.VMEM((C, 3 * HALF), BF),
            pltpu.VMEM((C, B), F32),
            pltpu.SemaphoreType.DMA((7,)),
            pltpu.SemaphoreType.DMA((2 * tiles,)),
        ],
        out_shape=[out, out],
        compiler_params=pltpu.CompilerParams(vmem_limit_bytes=24 * 1024 * 1024),
        name="update",
    )(owner, *near, *stay(inverse, offsets))


def shards(features, residual, coeffs, inverse, owner, offsets):
    swap = [(0, 1), (1, 0)]
    (owner,) = stay(owner)
    own, sib, owner = pick(owner, features, residual, inverse, offsets)
    owner = pltpu.with_memory_space_constraint(owner, pltpu.SMEM)
    half = small(half_kernel, GROUPS, owner, own, lax.ppermute(sib, "c", swap))
    part = lax.all_to_all(half, SPREAD, 0, 0, tiled=True)
    part = small(functools.partial(choose_kernel, 0), 4, owner, part)
    part = lax.all_to_all(part, "zh", 0, 0, tiled=True)
    part = small(functools.partial(choose_kernel, 1), GROUPS, owner, part)
    own = lax.all_to_all(part, SPREAD, 0, 0, tiled=True)
    sib = lax.ppermute(own, "c", swap)
    held = early(own, features, residual, coeffs)
    return update(owner, sib, *held, inverse, offsets)


def solution(mesh):
    fine = Mesh(mesh.devices.reshape(2, 4, 2, 4, 2, 2), AXES)
    cols = P(None, AXES)
    return jax.shard_map(
        shards,
        mesh=fine,
        in_specs=(cols, cols, cols, P(), P(), P()),
        out_specs=(cols, cols),
        check_vma=False,
    )
```
